32 devices in a mesh: blk: 4 (over x, core), rows: 8 (over z, y).
Axes of the slice: x: 2, y: 2, z: 4, core: 2. Of those that a mesh axis runs over, the one named last changes fastest.
Arguments:
- fock_band: bfloat16 [8192, 2176], P('rows'), may hold values from -0.125 to 0.125
- fock_slot_mask: int32 [64, 17], P('rows'), may hold values from 0 to 1, as said below
- orbital_slab: bfloat16 [8192, 2048], P('rows', 'blk'), may hold values from -6 to 6
- orbital_mask: int32 [64, 16], P('rows', 'blk'), may hold values 0 or 1
- result_mask: int32 [64, 16], P('rows', 'blk'), may hold values 0 or 1
Outputs:
- product_slab: bfloat16 [8192, 2048], P('rows', 'blk')
- projected: float32 [2048, 2048], P('rows', 'blk')
The draws below stay inside these ranges and needn't reach their ends.
Inputs may be any that keep to these rules, and one draw needn't show every extreme that they name: `fock_slot_mask`: 1 marks a present block slot.
All inputs are finite; a program needn't handle non-finite values. No bound on the sum of `orbital_mask` or of `result_mask` on one device may be relied on, other than what follows from the above.
Results may differ from the reference program's by a relative error of at most 0.0029.
Values may be sent and summed in bfloat16 or wider, within the bound.
A program may use at most 64 MiB of HBM per device.

```python
import math
import jax
import jax.numpy as jnp
from jax import lax

BLOCK = 128
BAND = 17
NB = 64
ORDER = 8192
SLAB = 2048


def draw_fock_slot_mask(key, part):
    levels = jax.random.randint(key, (NB, BAND), 0, 64)
    row_position = lax.broadcasted_iota(jnp.int32, (NB, BAND), 0)
    row_limit = 16 + 48 * row_position // NB
    return (levels < row_limit).astype(jnp.int32)


def plant(array, key, least, top_value):
    longest = array.shape.index(max(array.shape))
    spots = []
    for shift in (0, 1):
        where = [jax.random.randint(jax.random.fold_in(key, axis), (), 0, length) for axis, length in enumerate(array.shape)]
        where[longest] = (where[longest] + shift) % array.shape[longest]
        spots.append(tuple(where))
    return array.at[spots[0]].set(least).at[spots[1]].set(top_value)


def spiked(result, stream_key, source, target, shards_of, factor):
    def block_of(position):
        return (jnp.arange(result.shape[position]) // (result.shape[position] // shards_of)).reshape((-1,) + (1,) * (result.ndim - 1 - position))

    near = jax.random.permutation(stream_key, shards_of)[block_of(target)]
    second = (block_of(target) + shards_of // 2) % shards_of
    return jnp.where((block_of(source) == near) | (block_of(source) == second), factor * result, result)


def block_scale(own_key, shape, cuts, smallest, high):
    gain, own = 1.0, jax.random.fold_in(own_key, 6)
    for dim, shards_of in cuts:
        draws = jnp.exp(jax.random.uniform(jax.random.fold_in(own, dim), (shards_of,), jnp.float32, smallest / len(cuts), high / len(cuts)))
        gain = gain * jnp.repeat(draws, shape[dim] // shards_of).reshape([-1 if axis == dim else 1 for axis in range(len(shape))])
    return gain


def bell_draw(rng, extent, width, reach, shards=(), dtype=jnp.bfloat16):
    result = width * jax.random.normal(rng, extent, jnp.float32)
    if shards:
        result = result * block_scale(rng, extent, shards, -0.22, 0.18)
    return jnp.clip(result, -reach, reach).astype(dtype)


def heavy_noise(key, shape, deviation, most, pieces, heavy, kind=jnp.bfloat16):
    array = deviation * jax.random.normal(key, shape, jnp.float32)
    if pieces:
        array = array * block_scale(key, shape, pieces, -0.22, 0.18)
    return jnp.clip(spiked(array, jax.random.fold_in(key, 3), *heavy), -most, most).astype(kind)


def setup_inputs(seed: int = 0) -> dict:
    arg_keys = jax.random.split(jax.random.key(seed), 6)
    fock_band = bell_draw(arg_keys[0], (ORDER, BAND * BLOCK), (BAND * BLOCK) ** -0.5, 0.125, ((0, 8),))
    fock_slot_mask = draw_fock_slot_mask(jax.random.fold_in(arg_keys[5], 71), 0)
    orbital_slab = heavy_noise(arg_keys[2], (ORDER, SLAB), 1.0, 6.0, ((0, 8), (1, 4)), (0, 1, 8, 2.0))
    orbital_mask = plant((jax.random.randint(arg_keys[3], (NB, SLAB // BLOCK), 0, 4) < 3).astype(jnp.int32), jax.random.fold_in(arg_keys[3], 1), 0, 1)
    result_mask = plant((jax.random.randint(arg_keys[4], (NB, SLAB // BLOCK), 0, 4) < 3).astype(jnp.int32), jax.random.fold_in(arg_keys[4], 1), 0, 1)
    return dict(fock_band=fock_band, fock_slot_mask=fock_slot_mask, orbital_slab=orbital_slab, orbital_mask=orbital_mask, result_mask=result_mask)


def reference(fock_band, fock_slot_mask, orbital_slab, orbital_mask, result_mask):
    radius = (BAND - 1) // 2
    col_blocks = SLAB // BLOCK
    fock_block_list = fock_band.reshape(NB, BLOCK, BAND, BLOCK) * fock_slot_mask[:, None, :, None].astype(jnp.bfloat16)
    slab_blocks = (orbital_slab.reshape(NB, BLOCK, col_blocks, BLOCK) * orbital_mask[:, None, :, None].astype(jnp.bfloat16)).reshape(NB, BLOCK, SLAB)
    summed_total = jnp.zeros((NB, BLOCK, SLAB), jnp.float32)
    for band_shift in range(BAND):
        band_window = jnp.roll(slab_blocks, radius - band_shift, axis=0)
        summed_total = summed_total + jnp.einsum('wnq,wqg->wng', fock_block_list[:, :, band_shift, :].astype(jnp.float32), band_window.astype(jnp.float32))
    product_slab = (summed_total.reshape(NB, BLOCK, col_blocks, BLOCK) * result_mask[:, None, :, None].astype(jnp.float32)).reshape(NB * BLOCK, SLAB).astype(jnp.bfloat16)
    slab_rows = slab_blocks.reshape(NB * BLOCK, SLAB)
    projected = jnp.dot(slab_rows.T, product_slab, preferred_element_type=jnp.float32) * (1.0 / math.sqrt(NB * BLOCK))
    return (product_slab, projected)
```

```python
import functools
import math

import jax
import jax.numpy as jnp
from jax import lax
from jax.experimental import pallas as pl
from jax.experimental.pallas import tpu as pltpu
from jax.sharding import PartitionSpec as P

CHUNK = 256
MESH = pl.DeviceIdType.MESH


def scaled(block, flag):
    return block * jnp.full(block.shape, flag.astype(jnp.float32)).astype(block.dtype)


def kernel(
    n, nb, fmask, omask, rmask, fock_hbm, slab, prod_hbm, proj,
    fraw, fpad, ext, prod, gat, acc, send_a, recv_a, send_b, recv_b,
    near_s, near_r, far_s, far_r, x_s, x_r, c_s, c_r, f_s, f_r,
    a_s, a_r, b_s, b_r, fock_sem, prod_sem,
):
    local_blocks, band = fmask.shape
    rows, columns = slab.shape
    bs = rows // local_blocks
    chunks = columns // CHUNK
    per_chunk = CHUNK // bs
    parts = near_s.shape[1]
    part = rows // parts
    half = n // 2
    per_panel = half // nb
    csz = columns * nb // n
    pan_rows = columns // 2

    r = lax.axis_index("rows")
    b = lax.axis_index("blk")
    par = lax.rem(r, 2)
    partner = r + 1 - 2 * par
    far_to = lax.rem(r + 2 - 4 * par + n, n)
    mine = r // 2
    my_pan = mine // per_panel
    my_sub = lax.rem(mine, per_panel)
    sibling = b + 1 - 2 * lax.rem(b, 2)
    across = lax.rem(b + 2, nb)

    def remote(src, dst, ssem, rsem, rows_to=None, blk_to=None):
        return pltpu.make_async_remote_copy(
            src_ref=src, dst_ref=dst, send_sem=ssem, recv_sem=rsem,
            device_id={"rows": r if rows_to is None else rows_to, "blk": b if blk_to is None else blk_to},
            device_id_type=MESH,
        )

    barrier = pltpu.get_barrier_semaphore()
    for to in (sibling, across):
        pl.semaphore_signal(barrier, inc=1, device_id={"rows": r, "blk": to}, device_id_type=MESH)
    pl.semaphore_signal(barrier, inc=1, device_id={"rows": partner, "blk": b}, device_id_type=MESH)
    for s in range(1, half):
        pl.semaphore_signal(
            barrier, inc=1, device_id={"rows": lax.rem(r + 2 * s, n), "blk": b}, device_id_type=MESH
        )

    fock_copy = pltpu.make_async_copy(fock_hbm, fraw, fock_sem)
    fock_copy.start()

    for k in range(chunks):
        for i in range(local_blocks):
            for w in range(per_chunk):
                j = k * per_chunk + w
                ext[k, rows + i * bs : rows + (i + 1) * bs, w * bs : (w + 1) * bs] = scaled(
                    slab[i * bs : (i + 1) * bs, j * bs : (j + 1) * bs], omask[i, j]
                )

    pl.semaphore_wait(barrier, 3 + half - 1)

    def at_rows(base, q):
        return pl.ds(pl.multiple_of(base + q * part, part), part)

    near_from = 2 * rows * (1 - par)
    near_to = 2 * rows * par
    near = [
        [
            remote(
                ext.at[k, pl.ds(rows + q * part, part), :], ext.at[k, at_rows(near_to, q), :],
                near_s.at[k, q], near_r.at[k, q], rows_to=partner,
            )
            for q in range(parts)
        ]
        for k in range(chunks)
    ]
    far = [
        [
            remote(
                ext.at[k, at_rows(near_from, q), :], ext.at[k, at_rows(near_to, q), :],
                far_s.at[k, q], far_r.at[k, q], rows_to=far_to,
            )
            for q in range(parts)
        ]
        for k in range(chunks)
    ]
    for k in range(chunks):
        for q in range(parts):
            near[k][q].start()

    grain = min(csz, bs)
    for j in range(columns // bs):
        k, w = j // per_chunk, j % per_chunk
        turned = ext[k, rows : 2 * rows, w * bs : (w + 1) * bs].T
        for g in range(bs // grain):
            c = j * bs + g * grain
            t = c // csz
            at = (t // 2) * csz + c % csz
            gat[b, t % 2, at : at + grain, :] = turned[g * grain : (g + 1) * grain, :]

    order = (1 - par, par)
    over_x = [remote(gat.at[b, p], gat.at[b, p], x_s.at[u], x_r.at[u], blk_to=across) for u, p in enumerate(order)]
    to_core = [remote(gat.at[b, p], gat.at[b, p], c_s.at[u], c_r.at[u], blk_to=sibling) for u, p in enumerate(order)]
    pass_on = [
        remote(gat.at[across, p], gat.at[across, p], f_s.at[u], f_r.at[u], blk_to=sibling)
        for u, p in enumerate(order)
    ]
    for u in range(2):
        over_x[u].start()
        to_core[u].start()

    fock_copy.wait()

    def mask_pair(pair, carry):
        for h in range(2):
            at = pl.ds(pl.multiple_of((2 * pair + h) * bs, bs), bs)
            pad = 0 if h else band * bs
            fpad[at, pad : pad + bs] = jnp.zeros((bs, bs), fpad.dtype)
            for o in range(band):
                fpad[at, (o + h) * bs : (o + h + 1) * bs] = scaled(
                    fraw[at, o * bs : (o + 1) * bs], fmask[2 * pair + h, o]
                )
        return carry

    lax.fori_loop(0, local_blocks // 2, mask_pair, 0)

    def forward(k, q):
        near[k][q].wait_recv()
        far[k][q].start()

    def product(k):
        for q in range(parts):
            far[k][q].wait_recv()

        def pair_rows(pair, carry):
            at = pl.ds(pl.multiple_of(2 * pair * bs, 2 * bs), 2 * bs)
            window = pl.ds(pl.multiple_of(2 * pair * bs, 2 * bs), (band + 1) * bs)
            total = jnp.dot(fpad[at, :], ext[k, window, :], preferred_element_type=jnp.float32)
            for h in range(2):
                for w in range(per_chunk):
                    flag = rmask[2 * pair + h, k * per_chunk + w].astype(jnp.float32)
                    prod[k, pl.ds(pl.multiple_of((2 * pair + h) * bs, bs), bs), w * bs : (w + 1) * bs] = (
                        total[h * bs : (h + 1) * bs, w * bs : (w + 1) * bs] * flag
                    ).astype(prod.dtype)
            return carry

        lax.fori_loop(0, local_blocks // 2, pair_rows, 0)
        pltpu.make_async_copy(prod.at[k], prod_hbm.at[:, pl.ds(k * CHUNK, CHUNK)], prod_sem.at[k]).start()

    pans = [lax.rem(my_pan + s, nb) for s in range(1, nb + 1)]
    swap = [
        [remote(send_a.at[k, pan], recv_a.at[k, pan], a_s.at[k, s], a_r.at[k, s], rows_to=partner)
         for s, pan in enumerate(pans)]
        for k in range(chunks)
    ]

    def project_theirs(k):
        for s, pan in enumerate(pans):
            send_a[k, pan] = jnp.dot(
                gat[pan, 1 - par], prod[k], preferred_element_type=jnp.float32
            ).astype(send_a.dtype)
            swap[k][s].start()

    def project_own(k):
        for pan in pans:
            acc[k, pan] = jnp.dot(gat[pan, par], prod[k], preferred_element_type=jnp.float32)

    spread = []

    def reduce_pairs(k):
        for s, pan in enumerate(pans):
            swap[k][s].wait_recv()
            total = acc[k, pan] + recv_a[k, pan].astype(jnp.float32)
            acc[k, pan] = total
            send_b[k, pan] = total.astype(send_b.dtype)
            last = s == nb - 1
            for t in range(1 if last else 0, per_panel):
                sub = lax.rem(my_sub + t, per_panel)
                to = pan * per_panel + sub
                slot = lax.rem(mine - to + half, half) - 1
                copy = remote(
                    send_b.at[k, pan, pl.ds(pl.multiple_of(sub * csz, csz), csz), :],
                    recv_b.at[k, slot], b_s.at[k, slot], b_r.at[k, slot], rows_to=2 * to + par,
                )
                copy.start()
                spread.append(copy)

    def finish(k):
        total = acc[k, my_pan, pl.ds(pl.multiple_of(my_sub * csz, csz), csz), :]
        for slot in range(half - 1):
            remote(
                send_b.at[k, my_pan, pl.ds(0, csz), :], recv_b.at[k, slot],
                b_s.at[k, slot], b_r.at[k, slot], rows_to=partner,
            ).wait_recv()
            total = total + recv_b[k, slot].astype(jnp.float32)
        proj[:, k * CHUNK : (k + 1) * CHUNK] = total * (1.0 / math.sqrt(rows * n))

    def panels_in(u):
        over_x[u].wait_recv()
        pass_on[u].start()

    for q in range(parts):
        forward(0, q)
    panels_in(0)
    for q in range(parts - 1):
        forward(1, q)
    product(0)
    forward(1, parts - 1)
    to_core[0].wait_recv()
    pass_on[0].wait_recv()
    project_theirs(0)
    panels_in(1)
    to_core[1].wait_recv()
    pass_on[1].wait_recv()
    project_own(0)
    product(1)
    project_theirs(1)
    project_own(1)
    for k in range(chunks):
        reduce_pairs(k)
    for k in range(chunks):
        finish(k)

    for k in range(chunks):
        for q in range(parts):
            near[k][q].wait_send()
            far[k][q].wait_send()
        for s in range(nb):
            swap[k][s].wait_send()
        pltpu.make_async_copy(prod.at[k], prod_hbm.at[:, pl.ds(k * CHUNK, CHUNK)], prod_sem.at[k]).wait()
    for u in range(2):
        over_x[u].wait_send()
        to_core[u].wait_send()
        pass_on[u].wait_send()
    for copy in spread:
        copy.wait_send()


def on_device(n, nb, fock_band, fock_slot_mask, orbital_slab, orbital_mask, result_mask):
    local_blocks, band = fock_slot_mask.shape
    rows, columns = orbital_slab.shape
    bs = rows // local_blocks
    chunks = columns // CHUNK
    parts = 2
    half = n // 2
    csz = columns * nb // n
    pan_rows = columns // 2
    bf16, f32 = jnp.bfloat16, jnp.float32
    dma = pltpu.SemaphoreType.DMA
    smem = pl.BlockSpec(memory_space=pltpu.SMEM)
    vmem = pl.BlockSpec(memory_space=pltpu.VMEM)
    hbm = pl.BlockSpec(memory_space=pl.ANY)
    return pl.pallas_call(
        functools.partial(kernel, n, nb),
        out_shape=(
            jax.ShapeDtypeStruct((rows, columns), bf16),
            jax.ShapeDtypeStruct((csz, columns), f32),
        ),
        in_specs=[smem, smem, smem, hbm, vmem],
        out_specs=(hbm, vmem),
        scratch_shapes=[
            pltpu.VMEM((rows, band * bs), bf16),
            pltpu.VMEM((rows, (band + 1) * bs), bf16),
            pltpu.VMEM((chunks, 3 * rows, CHUNK), bf16),
            pltpu.VMEM((chunks, rows, CHUNK), bf16),
            pltpu.VMEM((nb, 2, pan_rows, rows), bf16),
            pltpu.VMEM((chunks, nb, pan_rows, CHUNK), f32),
            pltpu.VMEM((chunks, nb, pan_rows, CHUNK), bf16),
            pltpu.VMEM((chunks, nb, pan_rows, CHUNK), bf16),
            pltpu.VMEM((chunks, nb, pan_rows, CHUNK), bf16),
            pltpu.VMEM((chunks, half - 1, csz, CHUNK), bf16),
            dma((chunks, parts)), dma((chunks, parts)), dma((chunks, parts)), dma((chunks, parts)),
            dma((2,)), dma((2,)), dma((2,)), dma((2,)), dma((2,)), dma((2,)),
            dma((chunks, nb)), dma((chunks, nb)),
            dma((chunks, half - 1)), dma((chunks, half - 1)),
            dma(()), dma((chunks,)),
        ],
        compiler_params=pltpu.CompilerParams(
            collective_id=0, has_side_effects=True, vmem_limit_bytes=50 * 1024 * 1024
        ),
        cost_estimate=pl.CostEstimate(
            flops=2 * rows * columns * (band * bs + columns * nb), bytes_accessed=8 * 2**20, transcendentals=0
        ),
    )(fock_slot_mask, orbital_mask, result_mask, fock_band, orbital_slab)


def solution(mesh):
    placed = (
        P("rows", None),
        P("rows", None),
        P("rows", "blk"),
        P("rows", "blk"),
        P("rows", "blk"),
    )
    return jax.shard_map(
        functools.partial(on_device, mesh.shape["rows"], mesh.shape["blk"]),
        mesh=mesh,
        in_specs=placed,
        out_specs=(P("rows", "blk"), P("rows", "blk")),
        check_vma=False,
    )
```

```python
import functools
import math

import jax
import jax.numpy as jnp
from jax import lax
from jax.experimental import pallas as pl
from jax.experimental.pallas import tpu as pltpu
from jax.sharding import PartitionSpec as P

CHUNK = 256
MESH = pl.DeviceIdType.MESH


def scaled(block, flag):
    return block * jnp.full(block.shape, flag.astype(jnp.float32)).astype(block.dtype)


def kernel(
    n, nb, fmask_hbm, omask_hbm, rmask_hbm, fock_hbm, slab_hbm, prod_hbm, proj,
    fmask, omask, rmask, slab, fraw, fpad, ext, prod, gat, acc,
    send_a, recv_a, send_b, recv_b, send_c, recv_c,
    near_s, near_r, far_s, far_r, x_s, x_r, c_s, c_r, f_s, f_r,
    a_s, a_r, b_s, b_r, d_s, d_r, fock_sem, mask_sem, slab_sem, prod_sem,
):
    local_blocks, band = fmask_hbm.shape
    rows, columns = slab_hbm.shape
    bs = rows // local_blocks
    chunks = columns // CHUNK
    per_chunk = CHUNK // bs
    parts = near_s.shape[1]
    part = rows // parts
    quarter = n // 4
    csz = columns * nb // n
    groups, brows, gsubs = acc.shape[2], acc.shape[3], acc.shape[3] // csz

    r = lax.axis_index("rows")
    b = lax.axis_index("blk")
    par = lax.rem(r, 2)
    bit = lax.rem(r // 2, 2)
    rest = r // 4
    partner = r + 1 - 2 * par
    second = r + 2 - 4 * bit
    far_to = lax.rem(r + 2 - 4 * par + n, n)
    far_from = lax.rem(r - 2 + 4 * par + n, n)
    my_group = rest // gsubs
    my_sub = lax.rem(rest, gsubs)
    sibling = b + 1 - 2 * lax.rem(b, 2)
    across = lax.rem(b + 2, nb)

    def remote(src, dst, ssem, rsem, rows_to=None, blk_to=None):
        return pltpu.make_async_remote_copy(
            src_ref=src, dst_ref=dst, send_sem=ssem, recv_sem=rsem,
            device_id={"rows": r if rows_to is None else rows_to, "blk": b if blk_to is None else blk_to},
            device_id_type=MESH,
        )

    barrier = pltpu.get_barrier_semaphore()
    for to in (sibling, across):
        pl.semaphore_signal(barrier, inc=1, device_id={"rows": r, "blk": to}, device_id_type=MESH)
    peers = [partner, far_to, far_from] + [lax.rem(r + 4 * s, n) for s in range(1, quarter)]
    for to in peers:
        pl.semaphore_signal(barrier, inc=1, device_id={"rows": to, "blk": b}, device_id_type=MESH)

    slab_copies = [
        pltpu.make_async_copy(slab_hbm.at[:, pl.ds(k * CHUNK, CHUNK)], slab.at[k], slab_sem.at[k])
        for k in range(chunks)
    ]
    mask_copies = [
        pltpu.make_async_copy(src, dst, mask_sem.at[m])
        for m, (src, dst) in enumerate(((omask_hbm, omask), (fmask_hbm, fmask), (rmask_hbm, rmask)))
    ]
    fock_copy = pltpu.make_async_copy(fock_hbm, fraw, fock_sem)
    for copy in [mask_copies[0]] + slab_copies + mask_copies[1:] + [fock_copy]:
        copy.start()
    mask_copies[0].wait()

    def mask_chunk(k):
        slab_copies[k].wait()
        for i in range(local_blocks):
            for w in range(per_chunk):
                ext[k, rows + i * bs : rows + (i + 1) * bs, w * bs : (w + 1) * bs] = scaled(
                    slab[k, i * bs : (i + 1) * bs, w * bs : (w + 1) * bs], omask[k * per_chunk + w, i]
                )

    mask_chunk(0)
    pl.semaphore_wait(barrier, 2 + len(peers))

    def at_rows(base, q):
        return pl.ds(pl.multiple_of(base + q * part, part), part)

    near_from = 2 * rows * (1 - par)
    near_to = 2 * rows * par
    near = [
        [
            remote(
                ext.at[k, pl.ds(rows + q * part, part), :], ext.at[k, at_rows(near_to, q), :],
                near_s.at[k, q], near_r.at[k, q], rows_to=partner,
            )
            for q in range(parts)
        ]
        for k in range(chunks)
    ]
    far = [
        [
            remote(
                ext.at[k, at_rows(near_from, q), :], ext.at[k, at_rows(near_to, q), :],
                far_s.at[k, q], far_r.at[k, q], rows_to=far_to,
            )
            for q in range(parts)
        ]
        for k in range(chunks)
    ]
    for k in range(chunks):
        if k:
            mask_chunk(k)
        for q in range(parts):
            near[k][q].start()

    grain = min(csz, bs)
    for j in range(columns // bs):
        k, w = j // per_chunk, j % per_chunk
        turned = ext[k, rows : 2 * rows, w * bs : (w + 1) * bs].T
        for g in range(bs // grain):
            c = j * bs + g * grain
            t = c // csz
            at = (t // 2 % 2) * brows + (t // 4) * csz + c % csz
            gat[b, t % 2, at : at + grain, :] = turned[g * grain : (g + 1) * grain, :]

    order = (1 - par, par)
    over_x = [remote(gat.at[b, p], gat.at[b, p], x_s.at[u], x_r.at[u], blk_to=across) for u, p in enumerate(order)]
    to_core = [remote(gat.at[b, p], gat.at[b, p], c_s.at[u], c_r.at[u], blk_to=sibling) for u, p in enumerate(order)]
    pass_on = [
        remote(gat.at[across, p], gat.at[across, p], f_s.at[u], f_r.at[u], blk_to=sibling)
        for u, p in enumerate(order)
    ]
    for u in range(2):
        over_x[u].start()
        to_core[u].start()

    for copy in mask_copies[1:] + [fock_copy]:
        copy.wait()

    def mask_pair(pair, carry):
        for h in range(2):
            at = pl.ds(pl.multiple_of((2 * pair + h) * bs, bs), bs)
            pad = 0 if h else band * bs
            fpad[at, pad : pad + bs] = jnp.zeros((bs, bs), fpad.dtype)
            for o in range(band):
                fpad[at, (o + h) * bs : (o + h + 1) * bs] = scaled(
                    fraw[at, o * bs : (o + 1) * bs], fmask[2 * pair + h, o]
                )
        return carry

    lax.fori_loop(0, local_blocks // 2, mask_pair, 0)

    def forward(k, q):
        near[k][q].wait_recv()
        far[k][q].start()

    def product(k):
        for q in range(parts):
            far[k][q].wait_recv()

        def pair_rows(pair, carry):
            at = pl.ds(pl.multiple_of(2 * pair * bs, 2 * bs), 2 * bs)
            window = pl.ds(pl.multiple_of(2 * pair * bs, 2 * bs), (band + 1) * bs)
            total = jnp.dot(fpad[at, :], ext[k, window, :], preferred_element_type=jnp.float32)
            for h in range(2):
                for w in range(per_chunk):
                    flag = rmask[k * per_chunk + w, 2 * pair + h].astype(jnp.float32)
                    prod[k, pl.ds(pl.multiple_of((2 * pair + h) * bs, bs), bs), w * bs : (w + 1) * bs] = (
                        total[h * bs : (h + 1) * bs, w * bs : (w + 1) * bs] * flag
                    ).astype(prod.dtype)
            return carry

        lax.fori_loop(0, local_blocks // 2, pair_rows, 0)
        pltpu.make_async_copy(prod.at[k], prod_hbm.at[:, pl.ds(k * CHUNK, CHUNK)], prod_sem.at[k]).start()

    order_g = [lax.rem(my_group + s, groups) for s in range(1, groups + 1)]
    blocks = [(other, s, bit + other * (1 - 2 * bit), g) for other in (1, 0) for s, g in enumerate(order_g)]

    def panel_rows(p, q, g):
        if brows == gat.shape[2]:
            return gat[2 * g + q, p]
        return gat[g, p, pl.ds(pl.multiple_of(q * brows, brows), brows), :]

    swap = [
        [remote(send_a.at[k, q, g], recv_a.at[k, q, g], a_s.at[k, x], a_r.at[k, x], rows_to=partner)
         for x, (_, _, q, g) in enumerate(blocks)]
        for k in range(chunks)
    ]
    pairs = [
        [remote(send_b.at[k, g], recv_b.at[k, g], b_s.at[k, s], b_r.at[k, s], rows_to=second)
         for s, g in enumerate(order_g)]
        for k in range(chunks)
    ]

    def project_theirs(k):
        for x, (_, _, q, g) in enumerate(blocks):
            send_a[k, q, g] = jnp.dot(
                panel_rows(1 - par, q, g), prod[k], preferred_element_type=jnp.float32
            ).astype(send_a.dtype)
            swap[k][x].start()

    def project_own(k):
        for _, _, q, g in blocks:
            acc[k, q, g] = jnp.dot(panel_rows(par, q, g), prod[k], preferred_element_type=jnp.float32)

    spread = []

    def reduce(k, x):
        other, s, q, g = blocks[x]
        swap[k][x].wait_recv()
        total = acc[k, q, g] + recv_a[k, q, g].astype(jnp.float32)
        if other:
            send_b[k, g] = total.astype(send_b.dtype)
            pairs[k][s].start()
            return
        pairs[k][s].wait_recv()
        total = total + recv_b[k, g].astype(jnp.float32)
        last = s == groups - 1
        if last:
            acc[k, q, g] = total
        if last and gsubs == 1:
            return
        send_c[k, g] = total.astype(send_c.dtype)
        for t in range(1 if last else 0, gsubs):
            sub = lax.rem(my_sub + t, gsubs)
            to = g * gsubs + sub
            slot = lax.rem(rest - to + quarter, quarter) - 1
            copy = remote(
                send_c.at[k, g, pl.ds(pl.multiple_of(sub * csz, csz), csz), :],
                recv_c.at[k, slot], d_s.at[k, slot], d_r.at[k, slot], rows_to=4 * to + 2 * bit + par,
            )
            copy.start()
            spread.append(copy)

    def finish(k):
        total = acc[k, bit, my_group, pl.ds(pl.multiple_of(my_sub * csz, csz), csz), :]
        for slot in range(quarter - 1):
            remote(
                send_c.at[k, my_group, pl.ds(0, csz), :], recv_c.at[k, slot],
                d_s.at[k, slot], d_r.at[k, slot], rows_to=partner,
            ).wait_recv()
            total = total + recv_c[k, slot].astype(jnp.float32)
        proj[:, k * CHUNK : (k + 1) * CHUNK] = total * (1.0 / math.sqrt(rows * n))

    def panels_in(u):
        over_x[u].wait_recv()
        pass_on[u].start()

    for q in range(parts):
        forward(0, q)
    panels_in(0)
    for q in range(parts - 1):
        forward(1, q)
    product(0)
    to_core[0].wait_recv()
    pass_on[0].wait_recv()
    project_theirs(0)
    forward(1, parts - 1)
    panels_in(1)
    to_core[1].wait_recv()
    pass_on[1].wait_recv()
    project_own(0)
    for x in range(groups):
        reduce(0, x)
    product(1)
    project_theirs(1)
    for x in range(groups, 2 * groups):
        reduce(0, x)
    project_own(1)
    for x in range(groups):
        reduce(1, x)
    finish(0)
    for x in range(groups, 2 * groups):
        reduce(1, x)
    finish(1)

    for k in range(chunks):
        for q in range(parts):
            near[k][q].wait_send()
            far[k][q].wait_send()
        for copy in swap[k] + pairs[k]:
            copy.wait_send()
        pltpu.make_async_copy(prod.at[k], prod_hbm.at[:, pl.ds(k * CHUNK, CHUNK)], prod_sem.at[k]).wait()
    for u in range(2):
        over_x[u].wait_send()
        to_core[u].wait_send()
        pass_on[u].wait_send()
    for copy in spread:
        copy.wait_send()


def on_device(n, nb, fock_band, fock_slot_mask, orbital_slab, orbital_mask, result_mask):
    local_blocks, band = fock_slot_mask.shape
    rows, columns = orbital_slab.shape
    bs = rows // local_blocks
    chunks = columns // CHUNK
    parts = 2
    quarter = n // 4
    csz = columns * nb // n
    pan_rows = columns // 2
    groups, brows = (nb // 2, pan_rows) if n == 2 * nb else (nb, pan_rows // 2)
    bf16, f32 = jnp.bfloat16, jnp.float32
    dma = pltpu.SemaphoreType.DMA
    vmem = pl.BlockSpec(memory_space=pltpu.VMEM)
    hbm = pl.BlockSpec(memory_space=pltpu.HBM)
    return pl.pallas_call(
        functools.partial(kernel, n, nb),
        out_shape=(
            jax.ShapeDtypeStruct((rows, columns), bf16),
            jax.ShapeDtypeStruct((csz, columns), f32),
        ),
        in_specs=[hbm] * 5,
        out_specs=(pl.BlockSpec(memory_space=pl.ANY), vmem),
        scratch_shapes=[
            pltpu.SMEM(fock_slot_mask.shape, jnp.int32),
            pltpu.SMEM(orbital_mask.shape[::-1], jnp.int32),
            pltpu.SMEM(result_mask.shape[::-1], jnp.int32),
            pltpu.VMEM((chunks, rows, CHUNK), bf16),
            pltpu.VMEM((rows, band * bs), bf16),
            pltpu.VMEM((rows, (band + 1) * bs), bf16),
            pltpu.VMEM((chunks, 3 * rows, CHUNK), bf16),
            pltpu.VMEM((chunks, rows, CHUNK), bf16),
            pltpu.VMEM((nb, 2, pan_rows, rows), bf16),
            pltpu.VMEM((chunks, 2, groups, brows, CHUNK), f32),
            pltpu.VMEM((chunks, 2, groups, brows, CHUNK), bf16),
            pltpu.VMEM((chunks, 2, groups, brows, CHUNK), bf16),
            pltpu.VMEM((chunks, groups, brows, CHUNK), bf16),
            pltpu.VMEM((chunks, groups, brows, CHUNK), bf16),
            pltpu.VMEM((chunks, groups, brows, CHUNK), bf16),
            pltpu.VMEM((chunks, quarter - 1, csz, CHUNK), bf16),
            dma((chunks, parts)), dma((chunks, parts)), dma((chunks, parts)), dma((chunks, parts)),
            dma((2,)), dma((2,)), dma((2,)), dma((2,)), dma((2,)), dma((2,)),
            dma((chunks, 2 * groups)), dma((chunks, 2 * groups)),
            dma((chunks, groups)), dma((chunks, groups)),
            dma((chunks, quarter - 1)), dma((chunks, quarter - 1)),
            dma(()), dma((3,)), dma((chunks,)), dma((chunks,)),
        ],
        compiler_params=pltpu.CompilerParams(
            collective_id=0, has_side_effects=True, vmem_limit_bytes=64 * 2**20 - 2**17
        ),
        cost_estimate=pl.CostEstimate(
            flops=2 * rows * columns * (band * bs + columns * nb), bytes_accessed=8 * 2**20, transcendentals=0
        ),
    )(fock_slot_mask, orbital_mask.T, result_mask.T, fock_band, orbital_slab)


def solution(mesh):
    placed = (
        P("rows", None),
        P("rows", None),
        P("rows", "blk"),
        P("rows", "blk"),
        P("rows", "blk"),
    )
    return jax.shard_map(
        functools.partial(on_device, mesh.shape["rows"], mesh.shape["blk"]),
        mesh=mesh,
        in_specs=placed,
        out_specs=(P("rows", "blk"), P("rows", "blk")),
        check_vma=False,
    )
```

```python
import functools
import math

import jax
import jax.numpy as jnp
from jax import lax
from jax.experimental import pallas as pl
from jax.experimental.pallas import tpu as pltpu
from jax.sharding import PartitionSpec as P

CHUNK = 256
MESH = pl.DeviceIdType.MESH


def scaled(block, flag):
    return block * jnp.full(block.shape, flag.astype(jnp.float32)).astype(block.dtype)


def kernel(
    n, nb, fmask_hbm, omask_hbm, rmask_hbm, fock_hbm, slab_hbm, prod_hbm, proj,
    fmask, omask, rmask, slab, fraw, fpad, ext, prod, gat, acc,
    send_a, recv_a, send_b, recv_b, send_c, recv_c,
    near_s, near_r, far_s, far_r, x_s, x_r, c_s, c_r, f_s, f_r,
    a_s, a_r, b_s, b_r, d_s, d_r, fock_sem, mask_sem, slab_sem, prod_sem,
):
    local_blocks, band = fmask_hbm.shape
    rows, columns = slab_hbm.shape
    bs = rows // local_blocks
    chunks = columns // CHUNK
    per_chunk = CHUNK // bs
    parts = near_s.shape[1]
    part = rows // parts
    quarter = n // 4
    csz = columns * nb // n
    groups, brows, gsubs = acc.shape[2], acc.shape[3], acc.shape[3] // csz

    r = lax.axis_index("rows")
    b = lax.axis_index("blk")
    par = lax.rem(r, 2)
    bit = lax.rem(r // 2, 2)
    rest = r // 4
    partner = r + 1 - 2 * par
    second = r + 2 - 4 * bit
    far_to = lax.rem(r + 2 - 4 * par + n, n)
    far_from = lax.rem(r - 2 + 4 * par + n, n)
    my_group = rest // gsubs
    my_sub = lax.rem(rest, gsubs)
    sibling = b + 1 - 2 * lax.rem(b, 2)
    across = lax.rem(b + 2, nb)

    def remote(src, dst, ssem, rsem, rows_to=None, blk_to=None):
        return pltpu.make_async_remote_copy(
            src_ref=src, dst_ref=dst, send_sem=ssem, recv_sem=rsem,
            device_id={"rows": r if rows_to is None else rows_to, "blk": b if blk_to is None else blk_to},
            device_id_type=MESH,
        )

    barrier = pltpu.get_barrier_semaphore()
    for to in (sibling, across):
        pl.semaphore_signal(barrier, inc=1, device_id={"rows": r, "blk": to}, device_id_type=MESH)
    peers = [partner, far_to, far_from] + [lax.rem(r + 4 * s, n) for s in range(1, quarter)]
    for to in peers:
        pl.semaphore_signal(barrier, inc=1, device_id={"rows": to, "blk": b}, device_id_type=MESH)

    slab_copies = [
        pltpu.make_async_copy(slab_hbm.at[:, pl.ds(k * CHUNK, CHUNK)], slab.at[k], slab_sem.at[k])
        for k in range(chunks)
    ]
    mask_copies = [
        pltpu.make_async_copy(src, dst, mask_sem.at[m])
        for m, (src, dst) in enumerate(((omask_hbm, omask), (fmask_hbm, fmask), (rmask_hbm, rmask)))
    ]
    fock_copy = pltpu.make_async_copy(fock_hbm, fraw, fock_sem)
    for copy in [mask_copies[0]] + slab_copies + mask_copies[1:] + [fock_copy]:
        copy.start()
    mask_copies[0].wait()

    def mask_chunk(k):
        slab_copies[k].wait()
        for i in range(local_blocks):
            for w in range(per_chunk):
                ext[k, rows + i * bs : rows + (i + 1) * bs, w * bs : (w + 1) * bs] = scaled(
                    slab[k, i * bs : (i + 1) * bs, w * bs : (w + 1) * bs], omask[k * per_chunk + w, i]
                )

    mask_chunk(0)
    pl.semaphore_wait(barrier, 2 + len(peers))

    def at_rows(base, q):
        return pl.ds(pl.multiple_of(base + q * part, part), part)

    near_from = 2 * rows * (1 - par)
    near_to = 2 * rows * par
    near = [
        [
            remote(
                ext.at[k, pl.ds(rows + q * part, part), :], ext.at[k, at_rows(near_to, q), :],
                near_s.at[k, q], near_r.at[k, q], rows_to=partner,
            )
            for q in range(parts)
        ]
        for k in range(chunks)
    ]
    far = [
        [
            remote(
                ext.at[k, at_rows(near_from, q), :], ext.at[k, at_rows(near_to, q), :],
                far_s.at[k, q], far_r.at[k, q], rows_to=far_to,
            )
            for q in range(parts)
        ]
        for k in range(chunks)
    ]
    for k in range(chunks):
        if k:
            mask_chunk(k)
        for q in range(parts):
            near[k][q].start()

    grain = min(csz, bs)
    for j in range(columns // bs):
        k, w = j // per_chunk, j % per_chunk
        turned = ext[k, rows : 2 * rows, w * bs : (w + 1) * bs].T
        for g in range(bs // grain):
            c = j * bs + g * grain
            t = c // csz
            at = (t // 2 % 2) * brows + (t // 4) * csz + c % csz
            gat[b, t % 2, at : at + grain, :] = turned[g * grain : (g + 1) * grain, :]

    order = (1 - par, par)
    over_x = [remote(gat.at[b, p], gat.at[b, p], x_s.at[u], x_r.at[u], blk_to=across) for u, p in enumerate(order)]
    to_core = [remote(gat.at[b, p], gat.at[b, p], c_s.at[u], c_r.at[u], blk_to=sibling) for u, p in enumerate(order)]
    pass_on = [
        remote(gat.at[across, p], gat.at[across, p], f_s.at[u], f_r.at[u], blk_to=sibling)
        for u, p in enumerate(order)
    ]
    for u in range(2):
        over_x[u].start()
        to_core[u].start()

    for copy in mask_copies[1:] + [fock_copy]:
        copy.wait()

    def mask_pair(pair, carry):
        for h in range(2):
            at = pl.ds(pl.multiple_of((2 * pair + h) * bs, bs), bs)
            pad = 0 if h else band * bs
            fpad[at, pad : pad + bs] = jnp.zeros((bs, bs), fpad.dtype)
            for o in range(band):
                fpad[at, (o + h) * bs : (o + h + 1) * bs] = scaled(
                    fraw[at, o * bs : (o + 1) * bs], fmask[2 * pair + h, o]
                )
        return carry

    lax.fori_loop(0, local_blocks // 2, mask_pair, 0)

    def forward(k, q):
        near[k][q].wait_recv()
        far[k][q].start()

    def product(k):
        for q in range(parts):
            far[k][q].wait_recv()

        def pair_rows(pair, carry):
            at = pl.ds(pl.multiple_of(2 * pair * bs, 2 * bs), 2 * bs)
            window = pl.ds(pl.multiple_of(2 * pair * bs, 2 * bs), (band + 1) * bs)
            total = jnp.dot(fpad[at, :], ext[k, window, :], preferred_element_type=jnp.float32)
            for h in range(2):
                for w in range(per_chunk):
                    flag = rmask[k * per_chunk + w, 2 * pair + h].astype(jnp.float32)
                    prod[k, pl.ds(pl.multiple_of((2 * pair + h) * bs, bs), bs), w * bs : (w + 1) * bs] = (
                        total[h * bs : (h + 1) * bs, w * bs : (w + 1) * bs] * flag
                    ).astype(prod.dtype)
            return carry

        lax.fori_loop(0, local_blocks // 2, pair_rows, 0)
        pltpu.make_async_copy(prod.at[k], prod_hbm.at[:, pl.ds(k * CHUNK, CHUNK)], prod_sem.at[k]).start()

    order_g = [lax.rem(my_group + s, groups) for s in range(1, groups + 1)]
    blocks = [(other, s, bit + other * (1 - 2 * bit), g) for other in (1, 0) for s, g in enumerate(order_g)]

    def panel_rows(p, q, g):
        if brows == gat.shape[2]:
            return gat[2 * g + q, p]
        return gat[g, p, pl.ds(pl.multiple_of(q * brows, brows), brows), :]

    swap = [
        [remote(send_a.at[k, q, g], recv_a.at[k, q, g], a_s.at[k, x], a_r.at[k, x], rows_to=partner)
         for x, (_, _, q, g) in enumerate(blocks)]
        for k in range(chunks)
    ]
    pairs = [
        [remote(send_b.at[k, g], recv_b.at[k, g], b_s.at[k, s], b_r.at[k, s], rows_to=second)
         for s, g in enumerate(order_g)]
        for k in range(chunks)
    ]

    def project_theirs(k):
        for x, (_, _, q, g) in enumerate(blocks):
            send_a[k, q, g] = jnp.dot(
                panel_rows(1 - par, q, g), prod[k], preferred_element_type=jnp.float32
            ).astype(send_a.dtype)
            swap[k][x].start()

    def project_own(k):
        for _, _, q, g in blocks:
            acc[k, q, g] = jnp.dot(panel_rows(par, q, g), prod[k], preferred_element_type=jnp.float32)

    spread = []

    def reduce(k, x):
        other, s, q, g = blocks[x]
        swap[k][x].wait_recv()
        total = acc[k, q, g] + recv_a[k, q, g].astype(jnp.float32)
        if other:
            send_b[k, g] = total.astype(send_b.dtype)
            pairs[k][s].start()
            return
        pairs[k][s].wait_recv()
        total = total + recv_b[k, g].astype(jnp.float32)
        last = s == groups - 1
        if last:
            acc[k, q, g] = total
        if last and gsubs == 1:
            return
        send_c[k, g] = total.astype(send_c.dtype)
        for t in range(1 if last else 0, gsubs):
            sub = lax.rem(my_sub + t, gsubs)
            to = g * gsubs + sub
            slot = lax.rem(rest - to + quarter, quarter) - 1
            copy = remote(
                send_c.at[k, g, pl.ds(pl.multiple_of(sub * csz, csz), csz), :],
                recv_c.at[k, slot], d_s.at[k, slot], d_r.at[k, slot], rows_to=4 * to + 2 * bit + par,
            )
            copy.start()
            spread.append(copy)

    def finish(k):
        total = acc[k, bit, my_group, pl.ds(pl.multiple_of(my_sub * csz, csz), csz), :]
        for slot in range(quarter - 1):
            remote(
                send_c.at[k, my_group, pl.ds(0, csz), :], recv_c.at[k, slot],
                d_s.at[k, slot], d_r.at[k, slot], rows_to=partner,
            ).wait_recv()
            total = total + recv_c[k, slot].astype(jnp.float32)
        proj[:, k * CHUNK : (k + 1) * CHUNK] = total * (1.0 / math.sqrt(rows * n))

    def panels_in(u):
        over_x[u].wait_recv()
        pass_on[u].start()

    for q in range(parts):
        forward(0, q)
    panels_in(0)
    forward(1, 0)
    product(0)
    forward(1, 1)
    to_core[0].wait_recv()
    pass_on[0].wait_recv()
    project_theirs(0)
    for q in range(2, parts):
        forward(1, q)
    panels_in(1)
    to_core[1].wait_recv()
    pass_on[1].wait_recv()
    project_own(0)
    for x in range(groups):
        reduce(0, x)
    product(1)
    project_theirs(1)
    for x in range(groups, 2 * groups):
        reduce(0, x)
    project_own(1)
    for x in range(groups):
        reduce(1, x)
    finish(0)
    for x in range(groups, 2 * groups):
        reduce(1, x)
    finish(1)

    for k in range(chunks):
        for q in range(parts):
            near[k][q].wait_send()
            far[k][q].wait_send()
        for copy in swap[k] + pairs[k]:
            copy.wait_send()
        pltpu.make_async_copy(prod.at[k], prod_hbm.at[:, pl.ds(k * CHUNK, CHUNK)], prod_sem.at[k]).wait()
    for u in range(2):
        over_x[u].wait_send()
        to_core[u].wait_send()
        pass_on[u].wait_send()
    for copy in spread:
        copy.wait_send()


def on_device(n, nb, fock_band, fock_slot_mask, orbital_slab, orbital_mask, result_mask):
    local_blocks, band = fock_slot_mask.shape
    rows, columns = orbital_slab.shape
    bs = rows // local_blocks
    chunks = columns // CHUNK
    parts = 4
    quarter = n // 4
    csz = columns * nb // n
    pan_rows = columns // 2
    groups, brows = (nb // 2, pan_rows) if n == 2 * nb else (nb, pan_rows // 2)
    bf16, f32 = jnp.bfloat16, jnp.float32
    dma = pltpu.SemaphoreType.DMA
    vmem = pl.BlockSpec(memory_space=pltpu.VMEM)
    hbm = pl.BlockSpec(memory_space=pltpu.HBM)
    return pl.pallas_call(
        functools.partial(kernel, n, nb),
        out_shape=(
            jax.ShapeDtypeStruct((rows, columns), bf16),
            jax.ShapeDtypeStruct((csz, columns), f32),
        ),
        in_specs=[hbm] * 5,
        out_specs=(pl.BlockSpec(memory_space=pl.ANY), vmem),
        scratch_shapes=[
            pltpu.SMEM(fock_slot_mask.shape, jnp.int32),
            pltpu.SMEM(orbital_mask.shape[::-1], jnp.int32),
            pltpu.SMEM(result_mask.shape[::-1], jnp.int32),
            pltpu.VMEM((chunks, rows, CHUNK), bf16),
            pltpu.VMEM((rows, band * bs), bf16),
            pltpu.VMEM((rows, (band + 1) * bs), bf16),
            pltpu.VMEM((chunks, 3 * rows, CHUNK), bf16),
            pltpu.VMEM((chunks, rows, CHUNK), bf16),
            pltpu.VMEM((nb, 2, pan_rows, rows), bf16),
            pltpu.VMEM((chunks, 2, groups, brows, CHUNK), f32),
            pltpu.VMEM((chunks, 2, groups, brows, CHUNK), bf16),
            pltpu.VMEM((chunks, 2, groups, brows, CHUNK), bf16),
            pltpu.VMEM((chunks, groups, brows, CHUNK), bf16),
            pltpu.VMEM((chunks, groups, brows, CHUNK), bf16),
            pltpu.VMEM((chunks, groups, brows, CHUNK), bf16),
            pltpu.VMEM((chunks, quarter - 1, csz, CHUNK), bf16),
            dma((chunks, parts)), dma((chunks, parts)), dma((chunks, parts)), dma((chunks, parts)),
            dma((2,)), dma((2,)), dma((2,)), dma((2,)), dma((2,)), dma((2,)),
            dma((chunks, 2 * groups)), dma((chunks, 2 * groups)),
            dma((chunks, groups)), dma((chunks, groups)),
            dma((chunks, quarter - 1)), dma((chunks, quarter - 1)),
            dma(()), dma((3,)), dma((chunks,)), dma((chunks,)),
        ],
        compiler_params=pltpu.CompilerParams(
            collective_id=0, has_side_effects=True, vmem_limit_bytes=62 * 2**20
        ),
        cost_estimate=pl.CostEstimate(
            flops=2 * rows * columns * (band * bs + columns * nb), bytes_accessed=8 * 2**20, transcendentals=0
        ),
    )(fock_slot_mask, orbital_mask.T, result_mask.T, fock_band, orbital_slab)


def solution(mesh):
    placed = (
        P("rows", None),
        P("rows", None),
        P("rows", "blk"),
        P("rows", "blk"),
        P("rows", "blk"),
    )
    return jax.shard_map(
        functools.partial(on_device, mesh.shape["rows"], mesh.shape["blk"]),
        mesh=mesh,
        in_specs=placed,
        out_specs=(P("rows", "blk"), P("rows", "blk")),
        check_vma=False,
    )
```

```python
import functools
import math

import jax
import jax.numpy as jnp
from jax import lax
from jax.experimental import pallas as pl
from jax.experimental.pallas import tpu as pltpu
from jax.sharding import PartitionSpec as P

CHUNK = 256
MESH = pl.DeviceIdType.MESH


def scaled(block, flag):
    return block * jnp.full(block.shape, flag.astype(jnp.float32)).astype(block.dtype)


def kernel(
    n, nb, fmask_hbm, omask_hbm, rmask_hbm, fock_hbm, slab_hbm, prod_hbm, proj,
    fmask, omask, rmask, slab, fraw, fpad, ext, prod, gat, acc,
    send_a, recv_a, send_b, recv_b, send_c, recv_c,
    near_s, near_r, far_s, far_r, x_s, x_r, c_s, c_r, f_s, f_r,
    a_s, a_r, b_s, b_r, d_s, d_r, fock_sem, mask_sem, slab_sem, prod_sem,
):
    local_blocks, band = fmask_hbm.shape
    rows, columns = slab_hbm.shape
    bs = rows // local_blocks
    chunks = columns // CHUNK
    per_chunk = CHUNK // bs
    parts = near_s.shape[1]
    part = rows // parts
    quarter = n // 4
    csz = columns * nb // n
    groups, brows, gsubs = acc.shape[2], acc.shape[3], acc.shape[3] // csz

    r = lax.axis_index("rows")
    b = lax.axis_index("blk")
    par = lax.rem(r, 2)
    bit = lax.rem(r // 2, 2)
    rest = r // 4
    partner = r + 1 - 2 * par
    second = r + 2 - 4 * bit
    far_to = lax.rem(r + 2 - 4 * par + n, n)
    far_from = lax.rem(r - 2 + 4 * par + n, n)
    my_group = rest // gsubs
    my_sub = lax.rem(rest, gsubs)
    sibling = b + 1 - 2 * lax.rem(b, 2)
    across = lax.rem(b + 2, nb)

    def remote(src, dst, ssem, rsem, rows_to=None, blk_to=None):
        return pltpu.make_async_remote_copy(
            src_ref=src, dst_ref=dst, send_sem=ssem, recv_sem=rsem,
            device_id={"rows": r if rows_to is None else rows_to, "blk": b if blk_to is None else blk_to},
            device_id_type=MESH,
        )

    barrier = pltpu.get_barrier_semaphore()
    for to in (sibling, across):
        pl.semaphore_signal(barrier, inc=1, device_id={"rows": r, "blk": to}, device_id_type=MESH)
    peers = [partner, far_to, far_from] + [lax.rem(r + 4 * s, n) for s in range(1, quarter)]
    for to in peers:
        pl.semaphore_signal(barrier, inc=1, device_id={"rows": to, "blk": b}, device_id_type=MESH)

    slab_copies = [
        pltpu.make_async_copy(slab_hbm.at[:, pl.ds(k * CHUNK, CHUNK)], slab.at[k], slab_sem.at[k])
        for k in range(chunks)
    ]
    mask_copies = [
        pltpu.make_async_copy(src, dst, mask_sem.at[m])
        for m, (src, dst) in enumerate(((omask_hbm, omask), (fmask_hbm, fmask), (rmask_hbm, rmask)))
    ]
    fock_copy = pltpu.make_async_copy(fock_hbm, fraw, fock_sem)
    for copy in [mask_copies[0]] + slab_copies + mask_copies[1:] + [fock_copy]:
        copy.start()
    mask_copies[0].wait()

    def mask_chunk(k):
        slab_copies[k].wait()
        for i in range(local_blocks):
            for w in range(per_chunk):
                ext[k, rows + i * bs : rows + (i + 1) * bs, w * bs : (w + 1) * bs] = scaled(
                    slab[k, i * bs : (i + 1) * bs, w * bs : (w + 1) * bs], omask[k * per_chunk + w, i]
                )

    mask_chunk(0)
    pl.semaphore_wait(barrier, 2 + len(peers))

    def at_rows(base, q):
        return pl.ds(pl.multiple_of(base + q * part, part), part)

    near_from = 2 * rows * (1 - par)
    near_to = 2 * rows * par
    near = [
        [
            remote(
                ext.at[k, pl.ds(rows + q * part, part), :], ext.at[k, at_rows(near_to, q), :],
                near_s.at[k, q], near_r.at[k, q], rows_to=partner,
            )
            for q in range(parts)
        ]
        for k in range(chunks)
    ]
    far = [
        [
            remote(
                ext.at[k, at_rows(near_from, q), :], ext.at[k, at_rows(near_to, q), :],
                far_s.at[k, q], far_r.at[k, q], rows_to=far_to,
            )
            for q in range(parts)
        ]
        for k in range(chunks)
    ]
    for k in range(chunks):
        if k:
            mask_chunk(k)
        for q in range(parts):
            near[k][q].start()

    grain = min(csz, bs)
    for j in range(columns // bs):
        k, w = j // per_chunk, j % per_chunk
        turned = ext[k, rows : 2 * rows, w * bs : (w + 1) * bs].T
        for g in range(bs // grain):
            c = j * bs + g * grain
            t = c // csz
            at = (t // 2 % 2) * brows + (t // 4) * csz + c % csz
            gat[b, t % 2, at : at + grain, :] = turned[g * grain : (g + 1) * grain, :]

    order = (1 - par, par)
    over_x = [remote(gat.at[b, p], gat.at[b, p], x_s.at[u], x_r.at[u], blk_to=across) for u, p in enumerate(order)]
    to_core = [remote(gat.at[b, p], gat.at[b, p], c_s.at[u], c_r.at[u], blk_to=sibling) for u, p in enumerate(order)]
    pass_on = [
        remote(gat.at[across, p], gat.at[across, p], f_s.at[u], f_r.at[u], blk_to=sibling)
        for u, p in enumerate(order)
    ]
    for u in range(2):
        over_x[u].start()
        to_core[u].start()

    for copy in mask_copies[1:] + [fock_copy]:
        copy.wait()

    def mask_pair(pair, carry):
        for h in range(2):
            at = pl.ds(pl.multiple_of((2 * pair + h) * bs, bs), bs)
            pad = 0 if h else band * bs
            fpad[at, pad : pad + bs] = jnp.zeros((bs, bs), fpad.dtype)
            for o in range(band):
                fpad[at, (o + h) * bs : (o + h + 1) * bs] = scaled(
                    fraw[at, o * bs : (o + 1) * bs], fmask[2 * pair + h, o]
                )
        return carry

    lax.fori_loop(0, local_blocks // 2, mask_pair, 0)

    def forward(k, q):
        near[k][q].wait_recv()
        far[k][q].start()

    def product(k):
        for q in range(parts):
            far[k][q].wait_recv()

        def pair_rows(pair, carry):
            at = pl.ds(pl.multiple_of(2 * pair * bs, 2 * bs), 2 * bs)
            window = pl.ds(pl.multiple_of(2 * pair * bs, 2 * bs), (band + 1) * bs)
            total = jnp.dot(fpad[at, :], ext[k, window, :], preferred_element_type=jnp.float32)
            for h in range(2):
                for w in range(per_chunk):
                    flag = rmask[k * per_chunk + w, 2 * pair + h].astype(jnp.float32)
                    prod[k, pl.ds(pl.multiple_of((2 * pair + h) * bs, bs), bs), w * bs : (w + 1) * bs] = (
                        total[h * bs : (h + 1) * bs, w * bs : (w + 1) * bs] * flag
                    ).astype(prod.dtype)
            return carry

        lax.fori_loop(0, local_blocks // 2, pair_rows, 0)
        pltpu.make_async_copy(prod.at[k], prod_hbm.at[:, pl.ds(k * CHUNK, CHUNK)], prod_sem.at[k]).start()

    order_g = [lax.rem(my_group + s, groups) for s in range(1, groups + 1)]
    blocks = [(other, s, bit + other * (1 - 2 * bit), g) for other in (1, 0) for s, g in enumerate(order_g)]

    def panel_rows(p, q, g):
        if brows == gat.shape[2]:
            return gat[2 * g + q, p]
        return gat[g, p, pl.ds(pl.multiple_of(q * brows, brows), brows), :]

    swap = [
        [remote(send_a.at[k, q, g], recv_a.at[k, q, g], a_s.at[k, x], a_r.at[k, x], rows_to=partner)
         for x, (_, _, q, g) in enumerate(blocks)]
        for k in range(chunks)
    ]
    pairs = [
        [remote(send_b.at[k, g], recv_b.at[k, g], b_s.at[k, s], b_r.at[k, s], rows_to=second)
         for s, g in enumerate(order_g)]
        for k in range(chunks)
    ]

    def project_theirs(k):
        for x, (_, _, q, g) in enumerate(blocks):
            send_a[k, q, g] = jnp.dot(
                panel_rows(1 - par, q, g), prod[k], preferred_element_type=jnp.float32
            ).astype(send_a.dtype)
            swap[k][x].start()

    def project_own(k):
        for _, _, q, g in blocks:
            acc[k, q, g] = jnp.dot(panel_rows(par, q, g), prod[k], preferred_element_type=jnp.float32)

    spread = []

    def reduce(k, x):
        other, s, q, g = blocks[x]
        swap[k][x].wait_recv()
        total = acc[k, q, g] + recv_a[k, q, g].astype(jnp.float32)
        if other:
            send_b[k, g] = total.astype(send_b.dtype)
            pairs[k][s].start()
            return
        pairs[k][s].wait_recv()
        total = total + recv_b[k, g].astype(jnp.float32)
        last = s == groups - 1
        if last:
            acc[k, q, g] = total
        if last and gsubs == 1:
            return
        send_c[k, g] = total.astype(send_c.dtype)
        for t in range(1 if last else 0, gsubs):
            sub = lax.rem(my_sub + t, gsubs)
            to = g * gsubs + sub
            slot = lax.rem(rest - to + quarter, quarter) - 1
            copy = remote(
                send_c.at[k, g, pl.ds(pl.multiple_of(sub * csz, csz), csz), :],
                recv_c.at[k, slot], d_s.at[k, slot], d_r.at[k, slot], rows_to=4 * to + 2 * bit + par,
            )
            copy.start()
            spread.append(copy)

    def finish(k):
        total = acc[k, bit, my_group, pl.ds(pl.multiple_of(my_sub * csz, csz), csz), :]
        for slot in range(quarter - 1):
            remote(
                send_c.at[k, my_group, pl.ds(0, csz), :], recv_c.at[k, slot],
                d_s.at[k, slot], d_r.at[k, slot], rows_to=partner,
            ).wait_recv()
            total = total + recv_c[k, slot].astype(jnp.float32)
        proj[:, k * CHUNK : (k + 1) * CHUNK] = total

    def panels_in(u):
        over_x[u].wait_recv()
        pass_on[u].start()

    for q in range(parts):
        forward(0, q)
    panels_in(0)
    forward(1, 0)
    product(0)
    forward(1, 1)
    to_core[0].wait_recv()
    pass_on[0].wait_recv()
    project_theirs(0)
    for q in range(2, parts):
        forward(1, q)
    panels_in(1)
    to_core[1].wait_recv()
    pass_on[1].wait_recv()
    project_own(0)
    for x in range(groups):
        reduce(0, x)
    product(1)
    project_theirs(1)
    for x in range(groups, 2 * groups):
        reduce(0, x)
    project_own(1)
    for x in range(groups):
        reduce(1, x)
    finish(0)
    for x in range(groups, 2 * groups):
        reduce(1, x)
    finish(1)

    for k in range(chunks):
        for q in range(parts):
            near[k][q].wait_send()
            far[k][q].wait_send()
        for copy in swap[k] + pairs[k]:
            copy.wait_send()
        pltpu.make_async_copy(prod.at[k], prod_hbm.at[:, pl.ds(k * CHUNK, CHUNK)], prod_sem.at[k]).wait()
    for u in range(2):
        over_x[u].wait_send()
        to_core[u].wait_send()
        pass_on[u].wait_send()
    for copy in spread:
        copy.wait_send()


def on_device(n, nb, fock_band, fock_slot_mask, orbital_slab, orbital_mask, result_mask):
    local_blocks, band = fock_slot_mask.shape
    rows, columns = orbital_slab.shape
    bs = rows // local_blocks
    chunks = columns // CHUNK
    parts = 4
    quarter = n // 4
    csz = columns * nb // n
    pan_rows = columns // 2
    groups, brows = (nb // 2, pan_rows) if n == 2 * nb else (nb, pan_rows // 2)
    bf16, f32 = jnp.bfloat16, jnp.float32
    dma = pltpu.SemaphoreType.DMA
    vmem = pl.BlockSpec(memory_space=pltpu.VMEM)
    hbm = pl.BlockSpec(memory_space=pltpu.HBM)
    product_slab, terms = pl.pallas_call(
        functools.partial(kernel, n, nb),
        out_shape=(
            jax.ShapeDtypeStruct((rows, columns), bf16),
            jax.ShapeDtypeStruct((csz, columns), f32),
        ),
        in_specs=[hbm] * 5,
        out_specs=(pl.BlockSpec(memory_space=pl.ANY), vmem),
        scratch_shapes=[
            pltpu.SMEM(fock_slot_mask.shape, jnp.int32),
            pltpu.SMEM(orbital_mask.shape[::-1], jnp.int32),
            pltpu.SMEM(result_mask.shape[::-1], jnp.int32),
            pltpu.VMEM((chunks, rows, CHUNK), bf16),
            pltpu.VMEM((rows, band * bs), bf16),
            pltpu.VMEM((rows, (band + 1) * bs), bf16),
            pltpu.VMEM((chunks, 3 * rows, CHUNK), bf16),
            pltpu.VMEM((chunks, rows, CHUNK), bf16),
            pltpu.VMEM((nb, 2, pan_rows, rows), bf16),
            pltpu.VMEM((chunks, 2, groups, brows, CHUNK), f32),
            pltpu.VMEM((chunks, 2, groups, brows, CHUNK), bf16),
            pltpu.VMEM((chunks, 2, groups, brows, CHUNK), bf16),
            pltpu.VMEM((chunks, groups, brows, CHUNK), bf16),
            pltpu.VMEM((chunks, groups, brows, CHUNK), bf16),
            pltpu.VMEM((chunks, groups, brows, CHUNK), bf16),
            pltpu.VMEM((chunks, quarter - 1, csz, CHUNK), bf16),
            dma((chunks, parts)), dma((chunks, parts)), dma((chunks, parts)), dma((chunks, parts)),
            dma((2,)), dma((2,)), dma((2,)), dma((2,)), dma((2,)), dma((2,)),
            dma((chunks, 2 * groups)), dma((chunks, 2 * groups)),
            dma((chunks, groups)), dma((chunks, groups)),
            dma((chunks, quarter - 1)), dma((chunks, quarter - 1)),
            dma(()), dma((3,)), dma((chunks,)), dma((chunks,)),
        ],
        compiler_params=pltpu.CompilerParams(
            collective_id=0, has_side_effects=True, vmem_limit_bytes=62 * 2**20
        ),
        cost_estimate=pl.CostEstimate(
            flops=2 * rows * columns * (band * bs + columns * nb), bytes_accessed=8 * 2**20, transcendentals=0
        ),
    )(fock_slot_mask, orbital_mask.T, result_mask.T, fock_band, orbital_slab)
    return product_slab, terms * (1.0 / math.sqrt(rows * n))


def solution(mesh):
    placed = (
        P("rows", None),
        P("rows", None),
        P("rows", "blk"),
        P("rows", "blk"),
        P("rows", "blk"),
    )
    return jax.shard_map(
        functools.partial(on_device, mesh.shape["rows"], mesh.shape["blk"]),
        mesh=mesh,
        in_specs=placed,
        out_specs=(P("rows", "blk"), P("rows", "blk")),
        check_vma=False,
    )
```
